32 devices in a mesh: row: 8 (over z, y), col: 4 (over x, core).
Axes of the slice: x: 2, y: 2, z: 4, core: 2. Of those that a mesh axis runs over, the one named last changes fastest.
Arguments:
- train_x: float32 [8192, 128], P('row'), may hold values from -6 to 6
- test_x: float32 [4096, 128], P('col'), may hold values from -6 to 6
- scales: float32 [128], replicated, may hold values from 3 to 96
- targets: float32 [8192], P('row')
- factor: float32 [8192, 2048], P('row', 'col'), as said below
- inverses: float32 [8192, 1024], P('row'), as said below
Outputs:
- back_solved: float32 [8192, 4096], P('row', 'col')
- explained: float32 [4096], P('col')
- mean: float32 [4096], P('col')
The draws below stay inside these ranges and needn't reach their ends.
Inputs may be any that keep to these rules, and one draw needn't show every extreme that they name: factor is zero where its block column is not below its block row: entry [i, c] is zero unless c // 1024 < i // 1024. Each diagonal block of inverses is lower triangular with a positive diagonal.
All inputs are finite; a program needn't handle non-finite values.
Results may differ from the reference program's by a relative error of at most 0.0003.
Values sent between devices are 32-bit elements; how exact they have to be, the bound alone decides.
A program may use at most 128 MiB of HBM per device.

```python
import math
import jax
import jax.numpy as jnp
from jax import lax

DIM = 128
PANELS = 2
BLOCK = 1024
NTRAIN = 8192
NTEST = 4096


def draw_targets(key, part):
    index = jnp.arange(NTRAIN, dtype=jnp.float32)
    rising = (1.0 + 2.0 * index / NTRAIN) / math.sqrt(NTRAIN)
    base = jax.random.normal(jax.random.fold_in(key, 11), (NTRAIN,), jnp.float32)
    return (base * rising).astype(jnp.float32)


def draw_factor(key, part):
    width = PANELS * BLOCK
    values = jax.random.normal(jax.random.fold_in(key, 21), (NTRAIN, width), jnp.float32)
    row_block = lax.broadcasted_iota(jnp.int32, (NTRAIN, width), 0) // BLOCK
    col_block = lax.broadcasted_iota(jnp.int32, (NTRAIN, width), 1) // BLOCK
    scaled = values * (1.2 / math.sqrt(NTRAIN))
    return jnp.where(col_block < row_block, scaled, 0.0).astype(jnp.float32)


def draw_inverses(key, part):
    first, second = jax.random.split(jax.random.fold_in(key, 31))
    inner = lax.broadcasted_iota(jnp.int32, (NTRAIN, BLOCK), 0) % BLOCK
    column = lax.broadcasted_iota(jnp.int32, (NTRAIN, BLOCK), 1)
    diagonal = jnp.exp(jax.random.uniform(first, (NTRAIN, BLOCK), jnp.float32, math.log(0.6), math.log(1.5)))
    lower = jax.random.normal(second, (NTRAIN, BLOCK), jnp.float32)
    lower = lower * (0.6 / math.sqrt(BLOCK))
    return jnp.where(column == inner, diagonal, jnp.where(column < inner, lower, 0.0)).astype(jnp.float32)


def level_of(rng, dims, cuts, low, top_value):
    factor_of, own = 1.0, jax.random.fold_in(rng, 6)
    for dim, shards_of in cuts:
        steps = jnp.exp(jax.random.uniform(jax.random.fold_in(own, dim), (shards_of,), jnp.float32, low / len(cuts), top_value / len(cuts)))
        factor_of = factor_of * jnp.repeat(steps, dims[dim] // shards_of).reshape([-1 if axis == dim else 1 for axis in range(len(dims))])
    return factor_of


def normal_values(key, dims, deviation, most, cuts=(), kind=jnp.bfloat16):
    entries = deviation * jax.random.normal(key, dims, jnp.float32)
    if cuts:
        entries = entries * level_of(key, dims, cuts, -0.22, 0.18)
    return jnp.clip(entries, -most, most).astype(kind)


def setup_inputs(seed: int = 0) -> dict:
    key_of = jax.random.split(jax.random.key(seed), 7)
    return {
        "train_x": normal_values(key_of[0], (NTRAIN, DIM), 1.0, 6.0, ((0, 8),), jnp.float32),
        "test_x": normal_values(key_of[1], (NTEST, DIM), 1.0, 6.0, ((0, 4),), jnp.float32),
        "scales": jnp.clip(jnp.exp(jax.random.uniform(key_of[2], (DIM,), jnp.float32, math.log(3.0), math.log(96.0))), 3.0, 96.0),
        "targets": draw_targets(jax.random.fold_in(key_of[6], 71), 0),
        "factor": draw_factor(jax.random.fold_in(key_of[6], 71), 0),
        "inverses": draw_inverses(jax.random.fold_in(key_of[6], 71), 0),
    }


def cross_kernel(train_x, test_x, scales):
    highest = lax.Precision.HIGHEST
    scaled_train = train_x / scales
    scaled_test = test_x / scales
    squared = (jnp.sum(scaled_train * scaled_train, axis=1)[:, None]
               + jnp.sum(scaled_test * scaled_test, axis=1)[None, :]
               - 2.0 * jnp.dot(scaled_train, scaled_test.T, precision=highest))
    return jnp.exp(-0.5 * squared)


def apply_blocks(inverses, matrix, transpose):
    nblocks = NTRAIN // BLOCK
    stacked = inverses.reshape(nblocks, BLOCK, BLOCK)
    pieces = matrix.reshape(nblocks, BLOCK, matrix.shape[1])
    if transpose:
        result = jnp.einsum("kji,kjt->kit", stacked, pieces, precision=lax.Precision.HIGHEST)
    else:
        result = jnp.einsum("kij,kjt->kit", stacked, pieces, precision=lax.Precision.HIGHEST)
    return result.reshape(matrix.shape)


def reference(train_x, test_x, scales, targets, factor, inverses):
    highest = lax.Precision.HIGHEST
    kernel = cross_kernel(train_x, test_x, scales)
    border = PANELS * BLOCK
    panel_w = jnp.zeros((border, NTEST), jnp.float32)
    for step in range(PANELS):
        lower = step * BLOCK
        upper = lower + BLOCK
        rhs = kernel[lower:upper] - jnp.dot(factor[lower:upper], panel_w, precision=highest)
        solved = jnp.dot(inverses[lower:upper], rhs, precision=highest)
        panel_w = panel_w.at[lower:upper].set(solved)
    residue = kernel - jnp.dot(factor, panel_w, precision=highest)
    whitened = apply_blocks(inverses, residue, False)
    back_solved = apply_blocks(inverses, whitened, True)
    back_solved = back_solved.at[:border].set(0.0)
    for step in reversed(range(PANELS)):
        lower = step * BLOCK
        upper = lower + BLOCK
        rhs = whitened[lower:upper] - jnp.dot(factor[:, lower:upper].T, back_solved, precision=highest)
        solved = jnp.dot(inverses[lower:upper].T, rhs, precision=highest)
        back_solved = back_solved.at[lower:upper].set(solved)
    explained = jnp.sum(whitened * whitened, axis=0) / NTRAIN
    mean = jnp.dot(targets, back_solved, precision=highest)
    return back_solved, explained, mean
```

```python
import jax
import jax.numpy as jnp
from jax import lax
from jax.sharding import PartitionSpec as P

CHUNKS = 4


def product(left, right):
    return jnp.dot(left, right, precision=lax.Precision.HIGH)


def transposed_product(left, right):
    return lax.dot_general(left, right, (((0,), (0,)), ((), ())), precision=lax.Precision.HIGH)


def kernel_rows(rows_x, scaled_test, scales):
    scaled_rows = rows_x / scales
    squared = (
        jnp.sum(scaled_rows * scaled_rows, axis=1)[:, None]
        + jnp.sum(scaled_test * scaled_test, axis=1)[None, :]
        - 2.0 * jnp.dot(scaled_rows, scaled_test.T, precision=lax.Precision.HIGHEST)
    )
    return jnp.exp(-0.5 * squared)


def local(train_x, test_x, scales, targets, factor, inverses):
    block = inverses.shape[0]
    parts = lax.axis_size("row")
    pairs = parts // 2
    position = lax.axis_index("row")
    even = position % 2 == 0
    head = position < 2
    swap = [(r, r ^ 1) for r in range(2, parts)]

    def lanes(source, target):
        return [(2 * source + lane, 2 * target + lane) for lane in range(2)]

    border = lax.all_gather(factor, "col", axis=1, tiled=True)
    first = border[:, :block]
    kernel = kernel_rows(train_x, test_x / scales, scales)
    width = kernel.shape[1] // CHUNKS
    kernels = [kernel[:, c * width : (c + 1) * width] for c in range(CHUNKS)]

    whites, solved, sums = [], [], []
    arrived = []
    for c in range(CHUNKS):
        start = product(inverses, kernels[c])
        from_zero = lax.ppermute(start, "row", [(0, 1)])
        second = product(inverses, kernels[c] - product(first, from_zero))
        moving = jnp.where(even, start, second)
        mine = jnp.zeros_like(moving)
        for hop in range(pairs - 1):
            moving = lax.ppermute(moving, "row", lanes(hop, hop + 1))
            mine = mine + moving
        arrived.append((from_zero, mine))
    for c in range(CHUNKS):
        from_zero, mine = arrived[c]
        other = lax.ppermute(mine, "row", swap)
        panel0 = jnp.where(head, from_zero, jnp.where(even, mine, other))
        panel1 = jnp.where(even, other, mine)
        panels = jnp.concatenate([panel0, panel1], axis=0)
        white = product(inverses, kernels[c] - product(border, panels))
        back = transposed_product(inverses, white)
        terms = transposed_product(border, jnp.where(head, 0.0, back))
        terms0, terms1 = terms[:block], terms[block:]
        sent = lax.ppermute(jnp.where(even, terms1, terms0), "row", swap)
        total = jnp.where(even, terms0, terms1) + sent
        for hop in range(pairs - 1, 0, -1):
            total = total + lax.ppermute(total, "row", lanes(hop, hop - 1))
        whites.append(white)
        solved.append(back)
        sums.append(total)
    outs = []
    for c in range(CHUNKS):
        rest = whites[c] - sums[c]
        last = transposed_product(inverses, rest)
        to_zero = lax.ppermute(transposed_product(first, last), "row", [(1, 0)])
        final = transposed_product(inverses, rest - to_zero)
        outs.append(jnp.where(head, final, solved[c]))
    back_solved = jnp.concatenate(outs, axis=1)
    squares = jnp.concatenate([jnp.sum(w * w, axis=0) for w in whites])
    weighted = jnp.sum(targets[:, None] * back_solved, axis=0)
    explained, mean = lax.psum((squares, weighted), "row")
    return (back_solved, explained / (block * parts), mean)


def solution(mesh):
    placed = (P("row", None), P("col", None), P(), P("row"), P("row", "col"), P("row", None))
    return jax.shard_map(
        local,
        mesh=mesh,
        in_specs=placed,
        out_specs=(P("row", "col"), P("col"), P("col")),
        check_vma=False,
    )
```

```python
import jax
import jax.numpy as jnp
from jax import lax
from jax.sharding import PartitionSpec as P

CHUNKS = 4


def product(left, right):
    return jnp.dot(left, right, precision=lax.Precision.HIGH)


def transposed_product(left, right):
    return lax.dot_general(left, right, (((0,), (0,)), ((), ())), precision=lax.Precision.HIGH)


def kernel_rows(rows_x, scaled_test, scales):
    scaled_rows = rows_x / scales
    squared = (
        jnp.sum(scaled_rows * scaled_rows, axis=1)[:, None]
        + jnp.sum(scaled_test * scaled_test, axis=1)[None, :]
        - 2.0 * jnp.dot(scaled_rows, scaled_test.T, precision=lax.Precision.HIGHEST)
    )
    return jnp.exp(-0.5 * squared)


def local(train_x, test_x, scales, targets, factor, inverses):
    block = inverses.shape[0]
    parts = lax.axis_size("row")
    pairs = parts // 2
    position = lax.axis_index("row")
    even = position % 2 == 0
    head = position < 2
    swap = [(r, r ^ 1) for r in range(2, parts)]

    def lanes(source, target):
        return [(2 * source + lane, 2 * target + lane) for lane in range(2)]

    border = lax.all_gather(factor, "col", axis=1, tiled=True)
    first = border[:, :block]
    kernel = kernel_rows(train_x, test_x / scales, scales)
    width = kernel.shape[1] // CHUNKS
    kernels = [kernel[:, c * width : (c + 1) * width] for c in range(CHUNKS)]

    pair = position // 2
    whites, solved, sums = [], [], []
    zeros, moving = [], []
    for c in range(CHUNKS):
        start = product(inverses, kernels[c])
        zeros.append(lax.ppermute(start, "row", [(0, 1)]))
        second = product(inverses, kernels[c] - product(first, zeros[c]))
        moving.append(jnp.where(even, start, second))
    arrived = [None] * CHUNKS
    others = {}

    def exchange(c):
        others[c] = lax.ppermute(arrived[c], "row", swap)

    got = None
    for step in range(CHUNKS + pairs - 2):
        active = [(p, step - p) for p in range(pairs - 1) if 0 <= step - p < CHUNKS]
        if got is None:
            sent = moving[step]
        elif step < CHUNKS:
            sent = jnp.where(pair == 0, moving[step], got)
        else:
            sent = got
        done = step - pairs
        if done in others:
            sent, others[done] = lax.optimization_barrier((sent, others[done]))
        got = lax.ppermute(sent, "row", [link for p, _ in active for link in lanes(p, p + 1)])
        for p, c in active:
            part = jnp.where(pair == p + 1, got, 0.0)
            arrived[c] = part if arrived[c] is None else arrived[c] + part
            if p == pairs - 2 and c < 2:
                exchange(c)
    def hop(step):
        active = [(p, step - (pairs - 1 - p)) for p in range(1, pairs)]
        active = [(p, c) for p, c in active if 0 <= c < CHUNKS]
        sent = sums[active[-1][1]]
        for p, c in active[:-1]:
            sent = jnp.where(pair == p, sums[c], sent)
        if step + 2 < CHUNKS:
            sent, others[step + 2] = lax.optimization_barrier((sent, others[step + 2]))
        got = lax.ppermute(sent, "row", [link for p, _ in active for link in lanes(p, p - 1)])
        for p, c in active:
            sums[c] = sums[c] + jnp.where(pair == p - 1, got, 0.0)
            if p == 1:
                finish(c)

    def finish(c):
        rest = whites[c] - sums[c]
        last = transposed_product(inverses, rest)
        to_zero = lax.ppermute(transposed_product(first, last), "row", [(1, 0)])
        final = transposed_product(inverses, rest - to_zero)
        outs.append(jnp.where(head, final, solved[c]))

    outs = []
    for c in range(CHUNKS):
        from_zero, mine = zeros[c], arrived[c]
        other = others[c]
        panel0 = jnp.where(head, from_zero, jnp.where(even, mine, other))
        panel1 = jnp.where(even, other, mine)
        panels = jnp.concatenate([panel0, panel1], axis=0)
        white = product(inverses, kernels[c] - product(border, panels))
        back = transposed_product(inverses, white)
        terms = transposed_product(border, jnp.where(head, 0.0, back))
        terms0, terms1 = terms[:block], terms[block:]
        sent = jnp.where(even, terms1, terms0)
        if c + 2 < CHUNKS:
            sent, arrived[c + 2] = lax.optimization_barrier((sent, arrived[c + 2]))
        got = lax.ppermute(sent, "row", swap)
        if c + 2 < CHUNKS:
            exchange(c + 2)
        whites.append(white)
        solved.append(back)
        sums.append(jnp.where(even, terms0, terms1) + got)
        if c >= 1:
            hop(c - 1)
    for step in range(CHUNKS - 1, CHUNKS + pairs - 2):
        hop(step)
    back_solved = jnp.concatenate(outs, axis=1)
    squares = jnp.concatenate([jnp.sum(w * w, axis=0) for w in whites])
    weighted = jnp.sum(targets[:, None] * back_solved, axis=0)
    explained, mean = lax.psum((squares, weighted), "row")
    return (back_solved, explained / (block * parts), mean)


def solution(mesh):
    placed = (P("row", None), P("col", None), P(), P("row"), P("row", "col"), P("row", None))
    return jax.shard_map(
        local,
        mesh=mesh,
        in_specs=placed,
        out_specs=(P("row", "col"), P("col"), P("col")),
        check_vma=False,
    )
```

```python
import jax
import jax.numpy as jnp
from jax import lax
from jax.sharding import PartitionSpec as P

CHUNKS = 8


def product(left, right):
    return jnp.dot(left, right, precision=lax.Precision.HIGH)


def transposed_product(left, right):
    return lax.dot_general(left, right, (((0,), (0,)), ((), ())), precision=lax.Precision.HIGH)


def kernel_rows(rows_x, scaled_test, scales):
    scaled_rows = rows_x / scales
    squared = (
        jnp.sum(scaled_rows * scaled_rows, axis=1)[:, None]
        + jnp.sum(scaled_test * scaled_test, axis=1)[None, :]
        - 2.0 * jnp.dot(scaled_rows, scaled_test.T, precision=lax.Precision.HIGHEST)
    )
    return jnp.exp(-0.5 * squared)


def local(train_x, test_x, scales, targets, factor, inverses):
    block = inverses.shape[0]
    parts = lax.axis_size("row")
    pairs = parts // 2
    position = lax.axis_index("row")
    even = position % 2 == 0
    head = position < 2
    swap = [(r, r ^ 1) for r in range(2, parts)]

    def lanes(source, target):
        return [(2 * source + lane, 2 * target + lane) for lane in range(2)]

    border = lax.all_gather(factor, "col", axis=1, tiled=True)
    first = border[:, :block]
    kernel = kernel_rows(train_x, test_x / scales, scales)
    width = kernel.shape[1] // CHUNKS
    kernels = [kernel[:, c * width : (c + 1) * width] for c in range(CHUNKS)]

    pair = position // 2
    whites, solved, sums = [], [], []
    zeros, moving = [], []
    for c in range(CHUNKS):
        start = product(inverses, kernels[c])
        zeros.append(lax.ppermute(start, "row", [(0, 1)]))
        second = product(inverses, kernels[c] - product(first, zeros[c]))
        moving.append(jnp.where(even, start, second))
    arrived = [None] * CHUNKS
    others = {}

    def exchange(c):
        others[c] = lax.ppermute(arrived[c], "row", swap)

    got = None
    for step in range(CHUNKS + pairs - 2):
        active = [(p, step - p) for p in range(pairs - 1) if 0 <= step - p < CHUNKS]
        if got is None:
            sent = moving[step]
        elif step < CHUNKS:
            sent = jnp.where(pair == 0, moving[step], got)
        else:
            sent = got
        done = step - pairs
        if done in others:
            sent, others[done] = lax.optimization_barrier((sent, others[done]))
        got = lax.ppermute(sent, "row", [link for p, _ in active for link in lanes(p, p + 1)])
        for p, c in active:
            part = jnp.where(pair == p + 1, got, 0.0)
            arrived[c] = part if arrived[c] is None else arrived[c] + part
            if p == pairs - 2 and c < 2:
                exchange(c)
    def hop(step):
        active = [(p, step - (pairs - 1 - p)) for p in range(1, pairs)]
        active = [(p, c) for p, c in active if 0 <= c < CHUNKS]
        sent = sums[active[-1][1]]
        for p, c in active[:-1]:
            sent = jnp.where(pair == p, sums[c], sent)
        if step + 2 < CHUNKS:
            sent, others[step + 2] = lax.optimization_barrier((sent, others[step + 2]))
        got = lax.ppermute(sent, "row", [link for p, _ in active for link in lanes(p, p - 1)])
        for p, c in active:
            sums[c] = sums[c] + jnp.where(pair == p - 1, got, 0.0)
            if p == 1:
                finish(c)

    def finish(c):
        rest = whites[c] - sums[c]
        last = transposed_product(inverses, rest)
        to_zero = lax.ppermute(transposed_product(first, last), "row", [(1, 0)])
        final = transposed_product(inverses, rest - to_zero)
        outs.append(jnp.where(head, final, solved[c]))

    outs = []
    for c in range(CHUNKS):
        from_zero, mine = zeros[c], arrived[c]
        other = others[c]
        panel0 = jnp.where(head, from_zero, jnp.where(even, mine, other))
        panel1 = jnp.where(even, other, mine)
        panels = jnp.concatenate([panel0, panel1], axis=0)
        white = product(inverses, kernels[c] - product(border, panels))
        back = transposed_product(inverses, white)
        terms = transposed_product(border, jnp.where(head, 0.0, back))
        terms0, terms1 = terms[:block], terms[block:]
        sent = jnp.where(even, terms1, terms0)
        if c + 2 < CHUNKS:
            sent, arrived[c + 2] = lax.optimization_barrier((sent, arrived[c + 2]))
        got = lax.ppermute(sent, "row", swap)
        if c + 2 < CHUNKS:
            exchange(c + 2)
        whites.append(white)
        solved.append(back)
        sums.append(jnp.where(even, terms0, terms1) + got)
        if c >= 1:
            hop(c - 1)
    for step in range(CHUNKS - 1, CHUNKS + pairs - 2):
        hop(step)
    back_solved = jnp.concatenate(outs, axis=1)
    squares = jnp.concatenate([jnp.sum(w * w, axis=0) for w in whites])
    weighted = jnp.sum(targets[:, None] * back_solved, axis=0)
    explained, mean = lax.psum((squares, weighted), "row")
    return (back_solved, explained / (block * parts), mean)


def solution(mesh):
    placed = (P("row", None), P("col", None), P(), P("row"), P("row", "col"), P("row", None))
    return jax.shard_map(
        local,
        mesh=mesh,
        in_specs=placed,
        out_specs=(P("row", "col"), P("col"), P("col")),
        check_vma=False,
    )
```
